32 devices in a mesh: grp: 2 (over x), src: 8 (over z, y), tgt: 2 (over core).
Axes of the slice: x: 2, y: 2, z: 4, core: 2. Of those that a mesh axis runs over, the one named last changes fastest.
Arguments:
- sources: bfloat16 [2048, 64, 256], P(('grp', 'src', 'tgt')), parts along dimension 0, may hold values from -6 to 6
- warp: bfloat16 [2048], P(('grp', 'src', 'tgt')), parts along dimension 0, may hold values from 0.5 to 2
- interp: bfloat16 [2, 2, 64, 64], replicated, may hold values from -0.75 to 0.75
- omega: float32 [2, 2, 64, 64], replicated, may hold values from -8 to 8
- eval_interp: bfloat16 [64, 64], replicated, may hold values from -0.75 to 0.75
- eval_omega: float32 [64, 64], replicated, may hold values from -8 to 8
Outputs:
- values: float32 [2048, 64, 256], P(('grp', 'src', 'tgt')), parts along dimension 0
The draws below stay inside these ranges and needn't reach their ends.
There are 2 independent parts, one for each index of `grp`. The reference program is written for one: setup_inputs(seed, part) draws one part's arguments, and reference() takes and returns one part's arrays. A program takes and returns all parts, laid end to end along the dimension named above; an argument that names none is the same for every part. Nothing has to cross between parts.
All inputs are finite; a program needn't handle non-finite values.
Results may differ from the reference program's by a relative error of at most 0.012.
The reference program's roundings to bfloat16 on the way count: a program that leaves them out, or rounds other values in their place, can miss the bound.
Values may be sent and summed in bfloat16 or wider, within the bound.
No kernel may reach another device: no remote copies, remote signals or barrier semaphores. Data moves between devices by JAX's collectives and lax.ppermute only.
A program may use at most 64 MiB of HBM per device.

```python
import jax
import jax.numpy as jnp
from jax import lax

R = 64
F = 256
NB_DEV = 64
BOXES = 1024
N_SRC = 8


def block_scale(own_key, extent, split, least, high):
    level = 1.0
    for position, blocks in split:
        steps = jax.random.uniform(jax.random.fold_in(jax.random.fold_in(own_key, 6), position), (blocks,), jnp.float32, least / len(split), high / len(split))
        level = level * jnp.repeat(jnp.exp(steps), extent[position] // blocks).reshape((-1,) + (1,) * (len(extent) - 1 - position))
    return level


def centred(own_key, extent, scale, reach, shards=(), kind=jnp.bfloat16):
    factor_of = block_scale(own_key, extent, shards, -0.22, 0.18) if shards else 1.0
    array = jax.random.normal(own_key, extent, jnp.float32) * scale * factor_of
    return jnp.minimum(jnp.maximum(array, -reach), reach).astype(kind)


def setup_inputs(seed: int = 0, part: int = 0) -> dict:
    seeds = jax.random.split(jax.random.key(seed), 7)
    own_keys = jax.random.split(jax.random.fold_in(seeds[6], part), 7)
    sources = centred(own_keys[0], (BOXES, R, F), 1.0, 6.0, ((0, 16),))
    warp = jnp.clip(0.5 + 1.5 * jax.random.uniform(own_keys[1], (BOXES,), jnp.float32) ** block_scale(own_keys[1], (BOXES,), ((0, 16),), -0.2, 0.2), 0.5, 2.0).astype(jnp.bfloat16)
    interp = centred(seeds[2], (2, 2, R, R), R ** -0.5, 0.75)
    omega = jnp.clip(jax.random.uniform(seeds[3], (2, 2, R, R), jnp.float32, -8.0, 8.0), -8.0, 8.0)
    eval_interp = centred(seeds[4], (R, R), R ** -0.5, 0.75)
    eval_omega = jnp.clip(jax.random.uniform(seeds[5], (R, R), jnp.float32, -8.0, 8.0), -8.0, 8.0)
    return {"sources": sources, "warp": warp, "interp": interp, "omega": omega, "eval_interp": eval_interp, "eval_omega": eval_omega}


def level_tiles(interp, omega, child, warp, factor):
    pick = (child == 1)[:, None, None, None]
    gains = jnp.where(pick, interp[1][None], interp[0][None])
    freqs = jnp.where(pick, omega[1][None], omega[0][None])
    scaled = warp.astype(jnp.float32) * factor
    phase = freqs * scaled[:, None, None, None]
    return (gains.astype(jnp.float32) * jnp.cos(phase)).astype(jnp.bfloat16)


def combine(state, partner, tiles):
    own = jnp.einsum('bij,bjf->bif', tiles[:, 0].astype(jnp.float32), state.astype(jnp.float32))
    other = jnp.einsum('bij,bjf->bif', tiles[:, 1].astype(jnp.float32), partner.astype(jnp.float32))
    return (own + other).astype(jnp.bfloat16)


def reference(sources, warp, interp, omega, eval_interp, eval_omega):
    total = sources.shape[0]
    local_bits = NB_DEV.bit_length() - 1
    src_bits = N_SRC.bit_length() - 1
    order = list(range(local_bits)) + [local_bits + 1 + k for k in range(src_bits)] + [local_bits]
    block = min(512, total)
    blocks = total // block
    boxes = jnp.arange(total, dtype=jnp.int32)
    state = sources
    for level, bit in enumerate(order):
        half = 1 << bit
        partner = jnp.flip(state.reshape(total // (2 * half), 2, half, R, F), 1).reshape(total, R, F)
        child = (boxes >> bit) & 1
        factor = (level + 1) / 4.0

        def one_block(items, factor=factor):
            own, other, scales, sides = items
            tiles = level_tiles(interp, omega, sides, scales, factor)
            return combine(own, other, tiles)

        state = lax.map(one_block, (state.reshape(blocks, block, R, F), partner.reshape(blocks, block, R, F),
                                    warp.reshape(blocks, block), child.reshape(blocks, block))).reshape(total, R, F)

    def evaluate(items):
        own, scales = items
        phase = eval_omega[None] * scales.astype(jnp.float32)[:, None, None]
        tiles = (eval_interp.astype(jnp.float32)[None] * jnp.cos(phase)).astype(jnp.bfloat16)
        return jnp.einsum('bij,bjf->bif', tiles.astype(jnp.float32), own.astype(jnp.float32))

    values = lax.map(evaluate, (state.reshape(blocks, block, R, F), warp.reshape(blocks, block)))
    return values.reshape(total, R, F)
```

```python
import functools
import math

import jax
import jax.numpy as jnp
from jax import lax
from jax.experimental import pallas as pl
from jax.experimental.pallas import tpu as pltpu
from jax.sharding import PartitionSpec as P

CHUNK_BITS = 1
UNROLL = 16
VMEM_LIMIT = 56 * 1024 * 1024
SMEM = pl.BlockSpec(memory_space=pltpu.SMEM)
VMEM = pl.BlockSpec(memory_space=pltpu.VMEM)
ANY = pl.BlockSpec(memory_space=pl.ANY)
SINE = (6.28318516, -41.34165503, 81.60100405, -76.54978181, 39.53670223)
LANES = 128


def tile(gains, turns, scale):
    t = turns * scale
    u = t - jnp.round(t)
    z = 0.25 - jnp.abs(u)
    v = z * z
    poly = SINE[-1]
    for coefficient in SINE[-2::-1]:
        poly = poly * v + coefficient
    return (gains * z * poly).astype(jnp.bfloat16)


def product(tiles, state):
    return jnp.dot(tiles, state, preferred_element_type=jnp.float32)


def pair_tiles(gains, turns, first, second):
    rank = gains.shape[0] // 2
    return jnp.concatenate(
        [tile(gains[:rank], turns[:rank], first), tile(gains[rank:], turns[rank:], second)], axis=0
    )


def sweep(count, load, work, store):
    def batch(items):
        loaded = [load(i) for i in items]
        results = [work(i, x) for i, x in zip(items, loaded)]
        for i, result in zip(items, results):
            store(i, result)

    if count <= UNROLL:
        batch(range(count))
    else:

        @pl.loop(0, count // UNROLL)
        def _(step):
            batch([step * UNROLL + j for j in range(UNROLL)])


def split_pair(index, bit):
    low = index & ((1 << bit) - 1)
    return ((index >> bit) << (bit + 1)) | low


def stack_tables(interp_ref, omega_ref, gains, turns, flips):
    rank = interp_ref.shape[-1]
    for table, out, scale in ((interp_ref, gains, 1.0), (omega_ref, turns, 0.5 / math.pi)):
        for flip in range(flips):
            for row in range(2):
                child = row ^ flip
                for column in range(2):
                    part = table[child, row ^ column].astype(jnp.float32) * scale
                    out[flip, row * rank:(row + 1) * rank, column * rank:(column + 1) * rank] = part


def scale_rows(warp_ref, rows):
    count = rows.shape[0]
    warp = jnp.broadcast_to(warp_ref[...].astype(jnp.float32), (count, count))
    diagonal = lax.broadcasted_iota(jnp.int32, (count, count), 0) == lax.broadcasted_iota(jnp.int32, (count, count), 1)
    column = jnp.sum(jnp.where(diagonal, warp, 0.0), axis=1, keepdims=True)
    rows[...] = jnp.broadcast_to(column, rows.shape)


def row_of(rows, index):
    return rows[pl.ds(index, 1), :]


def local_kernel(chunk, chunk_bits, groups, place_ref, warp_ref, interp_ref, omega_ref, sources_hbm, *rest):
    outs = rest[:groups]
    sources_ref, state, gains, turns, rows, sem = rest[groups:]
    copy = pltpu.make_async_copy(sources_hbm, sources_ref, sem)
    copy.start()
    stack_tables(interp_ref, omega_ref, gains, turns, 1)
    scale_rows(warp_ref, rows)
    total, rank, width = sources_ref.shape
    bits = total.bit_length() - 1
    count = total >> chunk_bits
    place = place_ref[0]
    copy.wait()

    source, kept = sources_ref, total
    for level in range(chunk_bits):
        side = chunk >> level & 1
        kept = kept // 2
        factor = (level + 1) / 4.0
        half = slice(side * rank, (side + 1) * rank)

        def load(i, source=source):
            return jnp.concatenate([source[2 * i], source[2 * i + 1]], axis=0)

        def work(i, x, level=level, factor=factor, half=half):
            low = chunk & ((1 << (level + 1)) - 1)
            scale = row_of(rows, (i << (level + 1)) | low) * factor
            return product(tile(gains[0, half], turns[0, half], scale), x).astype(jnp.bfloat16)

        def store(i, y):
            state[i] = y

        sweep(kept, load, work, store)
        source = state

    for level in range(chunk_bits, bits):
        bit = level - chunk_bits
        factor = (level + 1) / 4.0

        def load(i, bit=bit, source=source):
            first = split_pair(i, bit)
            return jnp.concatenate([source[first], source[first | (1 << bit)]], axis=0)

        def work(i, x, bit=bit, factor=factor):
            first = split_pair(i, bit)
            boxes = [((first | (s << bit)) << chunk_bits) | chunk for s in range(2)]
            scales = [row_of(rows, b) * factor for b in boxes]
            return product(pair_tiles(gains[0], turns[0], *scales), x).astype(jnp.bfloat16)

        def store(i, y, bit=bit):
            first = split_pair(i, bit)
            state[first] = y[:rank]
            state[first | (1 << bit)] = y[rank:]

        sweep(count // 2, load, work, store)
        source = state

    part = count // groups
    for k in range(groups):
        group = place ^ k
        outs[k][:part * rank] = state[pl.ds(group * part, part)].reshape(part * rank, width)
        if chunk == 0:
            each = total // groups
            extra = outs[k].shape[0] - part * rank
            mine = rows[pl.ds(group * each, each), :]
            if extra > each:
                mine = jnp.concatenate([mine, jnp.zeros((extra - each, LANES), jnp.float32)], axis=0)
            mine = mine.astype(jnp.bfloat16)
            for lane in range(0, width, LANES):
                outs[k][part * rank:, lane:lane + LANES] = mine


def remote_kernel(chunk, chunk_bits, groups, first_level, part, place_ref, interp_ref, omega_ref, *rest):
    blocks, rest = rest[:groups], rest[groups:]
    if chunk:
        rows, out, gains, turns = rest
    else:
        out, rows, gains, turns = rest
    stack_tables(interp_ref, omega_ref, gains, turns, 2)
    count, rank, width = out.shape
    place = place_ref[0]
    group_bits = groups.bit_length() - 1
    part_bits = part.bit_length() - 1
    for k in range(groups):
        out[k * part:(k + 1) * part] = blocks[k][:part * rank].reshape(part, rank, width)
        if not chunk:
            extra = blocks[k].shape[0] - part * rank
            rows[k * extra:(k + 1) * extra, :] = blocks[k][part * rank:, :LANES].astype(jnp.float32)
    extra = rows.shape[0] // groups

    def scale_of(i, factor):
        k, m = i >> part_bits, i & (part - 1)
        return row_of(rows, k * extra + ((m << chunk_bits) | chunk)) * factor

    for step in range(group_bits):
        bit = step + part_bits
        factor = (first_level + step + 1) / 4.0
        side = place >> step & 1

        def load(i, bit=bit):
            first = split_pair(i, bit)
            return jnp.concatenate([out[first], out[first | (1 << bit)]], axis=0)

        def work(i, x, bit=bit, factor=factor, side=side):
            first = split_pair(i, bit)
            scales = [scale_of(first | (s << bit), factor) for s in range(2)]
            return product(pair_tiles(gains[side], turns[side], *scales), x).astype(jnp.bfloat16)

        def store(i, y, bit=bit):
            first = split_pair(i, bit)
            out[first] = y[:rank]
            out[first | (1 << bit)] = y[rank:]

        sweep(count // 2, load, work, store)


def core_kernel(chunk, chunk_bits, groups, level, core_ref, interp_ref, omega_ref, rows, own, other, *rest):
    outs, (gains, turns) = rest[:groups], rest[groups:]
    stack_tables(interp_ref, omega_ref, gains, turns, 2)
    count, rank, width = own.shape
    part = count // groups
    extra = rows.shape[0] // groups
    core = core_ref[0]
    factor = (level + 1) / 4.0
    for k in range(groups):

        def load(m, k=k):
            return jnp.concatenate([own[k * part + m], other[k * part + m]], axis=0)

        def work(m, x, k=k):
            scale = row_of(rows, k * extra + ((m << chunk_bits) | chunk)) * factor
            return product(tile(gains[core, :rank], turns[core, :rank], scale), x).astype(jnp.bfloat16)

        def store(m, y, k=k):
            outs[k][m * rank:(m + 1) * rank] = y

        sweep(part, load, work, store)


def eval_kernel(chunk, chunk_bits, groups, part, place_ref, warp_ref, interp_ref, omega_ref, *rest):
    blocks = rest[:groups]
    out_hbm, values, rows, sems = rest[-4:]
    rank, width = interp_ref.shape[-1], blocks[0].shape[-1]
    place = place_ref[0]
    scale_rows(warp_ref, rows)
    gains = interp_ref[...].astype(jnp.float32)
    turns = omega_ref[...] * (0.5 / math.pi)
    gains, turns = jnp.concatenate([gains, gains], axis=1), jnp.concatenate([turns, turns], axis=1)
    left = lax.broadcasted_iota(jnp.int32, (1, 2 * rank), 1) < rank
    for k in range(groups):
        group = place ^ k

        def scale_of(m):
            return row_of(rows, ((group * part + m) << chunk_bits) | chunk)

        for m in range(0, part, 2):
            if m + 1 < part:
                both = tile(gains, turns, jnp.where(left, scale_of(m), scale_of(m + 1)))
                none = jnp.zeros_like(both)
                tiles = jnp.concatenate([jnp.where(left, both, none), jnp.where(left, none, both)], axis=0)
                result = product(tiles, blocks[k][m * rank:(m + 2) * rank])
                values[k, m], values[k, m + 1] = result[:rank], result[rank:]
            else:
                tiles = tile(gains[:, :rank], turns[:, :rank], scale_of(m)[:, :rank])
                values[k, m] = product(tiles, blocks[k][m * rank:(m + 1) * rank])
        pltpu.make_async_copy(values.at[k], out_hbm.at[group, :, chunk], sems.at[k]).start()
    for k in range(groups):
        pltpu.make_async_copy(values.at[k], out_hbm.at[place ^ k, :, chunk], sems.at[k]).wait()


def on_device(sources, warp, interp, omega, eval_interp, eval_omega):
    total, rank, width = sources.shape
    bits = total.bit_length() - 1
    groups = lax.axis_size("src")
    group_bits = groups.bit_length() - 1
    chunk_bits = min(CHUNK_BITS, bits - group_bits)
    chunks = 1 << chunk_bits
    count = total // chunks
    part = count // groups
    extra = -(-total // groups // 16) * 16
    bf16, f32 = jnp.bfloat16, jnp.float32
    params = pltpu.CompilerParams(vmem_limit_bytes=VMEM_LIMIT)
    place = lax.axis_index("src").astype(jnp.int32).reshape(1)
    core = lax.axis_index("tgt").astype(jnp.int32).reshape(1)
    warp = warp.reshape(1, total)
    block = jax.ShapeDtypeStruct((part * rank, width), bf16)
    long_block = jax.ShapeDtypeStruct((part * rank + extra, width), bf16)
    tables = [pltpu.VMEM((1, 2 * rank, 2 * rank), f32)] * 2
    both_tables = [pltpu.VMEM((2, 2 * rank, 2 * rank), f32)] * 2
    row_shape = jax.ShapeDtypeStruct((groups * extra, LANES), f32)

    def cost(items, level_count):
        return pl.CostEstimate(
            flops=items * level_count * 40 * rank * rank * width,
            bytes_accessed=items * rank * width * 4,
            transcendentals=items * level_count * rank * rank,
        )

    far_first = sorted(range(1, groups), reverse=True)

    def spread(blocks):
        moved = {0: blocks[0]}
        for k in far_first:
            moved[k] = lax.ppermute(blocks[k], "src", [(i, i ^ k) for i in range(groups)])
        return [moved[k] for k in range(groups)]

    outgoing = []
    for chunk in range(chunks):
        outgoing.append(spread(pl.pallas_call(
            functools.partial(local_kernel, chunk, chunk_bits, groups),
            out_shape=[block if chunk else long_block] * groups,
            in_specs=[SMEM, VMEM, VMEM, VMEM, ANY],
            out_specs=[VMEM] * groups,
            scratch_shapes=[
                pltpu.VMEM((total, rank, width), bf16),
                pltpu.VMEM((max(total // 2, count), rank, width), bf16),
                *tables,
                pltpu.VMEM((total, LANES), f32),
                pltpu.SemaphoreType.DMA,
            ],
            compiler_params=params,
            cost_estimate=cost(count, bits),
            name=f"local_{chunk}",
        )(place, warp, interp, omega, sources)))
    returning = []
    rows = None
    for chunk in range(chunks):
        whole = jax.ShapeDtypeStruct((count, rank, width), bf16)
        result = pl.pallas_call(
            functools.partial(remote_kernel, chunk, chunk_bits, groups, bits, part),
            out_shape=whole if chunk else [whole, row_shape],
            in_specs=[SMEM, VMEM, VMEM] + [VMEM] * groups + [VMEM] * (chunk > 0),
            out_specs=VMEM if chunk else [VMEM, VMEM],
            scratch_shapes=both_tables,
            compiler_params=params,
            cost_estimate=cost(count, group_bits),
            name=f"remote_{chunk}",
        )(place, interp, omega, *outgoing[chunk], *([rows] if chunk else []))
        state, rows = (result, rows) if chunk else result
        other = lax.ppermute(state, "tgt", [(i, i ^ 1) for i in range(lax.axis_size("tgt"))])
        returning.append(spread(pl.pallas_call(
            functools.partial(core_kernel, chunk, chunk_bits, groups, bits + group_bits),
            out_shape=[block] * groups,
            in_specs=[SMEM, VMEM, VMEM, VMEM, VMEM, VMEM],
            out_specs=[VMEM] * groups,
            scratch_shapes=both_tables,
            compiler_params=params,
            cost_estimate=cost(count, 1),
            name=f"core_{chunk}",
        )(core, interp, omega, rows, state, other)))
    values = None
    for chunk in range(chunks):
        operands = [place, warp, eval_interp, eval_omega] + returning[chunk]
        specs = [SMEM, VMEM, VMEM, VMEM] + [VMEM] * groups
        aliases = {}
        if values is not None:
            aliases = {len(operands): 0}
            operands.append(values)
            specs.append(ANY)
        values = pl.pallas_call(
            functools.partial(eval_kernel, chunk, chunk_bits, groups, part),
            out_shape=jax.ShapeDtypeStruct((groups, part, chunks, rank, width), f32),
            in_specs=specs,
            out_specs=ANY,
            scratch_shapes=[
                pltpu.VMEM((groups, part, rank, width), f32),
                pltpu.VMEM((total, LANES), f32),
                pltpu.SemaphoreType.DMA((groups,)),
            ],
            input_output_aliases=aliases,
            compiler_params=params,
            cost_estimate=cost(count, 1),
            name=f"eval_{chunk}",
        )(*operands)
    return values.reshape(total, rank, width)


def solution(mesh):
    in_specs = (P(("grp", "src", "tgt"), None, None), P(("grp", "src", "tgt")), P(), P(), P(), P())
    out_specs = P(("grp", "src", "tgt"), None, None)
    return jax.shard_map(
        on_device, mesh=mesh, in_specs=in_specs, out_specs=out_specs, check_vma=False
    )
```

```python
import functools
import math

import jax
import jax.numpy as jnp
from jax import lax
from jax.experimental import pallas as pl
from jax.experimental.pallas import tpu as pltpu
from jax.sharding import PartitionSpec as P

BATCH = 16
GROUP_BITS = 3
HALVES = 2
VMEM_LIMIT = 20 * 1024 * 1024
WARP_ROWS = 16
VMEM = pl.BlockSpec(memory_space=pltpu.VMEM)
ANY = pl.BlockSpec(memory_space=pl.ANY)
HBM = pl.BlockSpec(memory_space=pltpu.HBM)
SINE = (6.28318516, -41.34165503, 81.60100405, -76.54978181, 39.53670223)
LANES = 128


def cosine(turns):
    u = turns - jnp.round(turns)
    z = 0.25 - jnp.abs(u)
    v = z * z
    poly = SINE[-1]
    for coefficient in SINE[-2::-1]:
        poly = poly * v + coefficient
    return z * poly


def tile(gains, turns, scale):
    return (gains * cosine(turns * scale)).astype(jnp.bfloat16)


def product(tiles, state):
    return jnp.dot(tiles, state, preferred_element_type=jnp.float32)


def split_pair(index, bit):
    low = index & ((1 << bit) - 1)
    return ((index >> bit) << (bit + 1)) | low


def pairs_of(count, bit):
    firsts = [split_pair(i, bit) for i in range(count // 2)]
    return [(i, first, first | (1 << bit)) for i, first in enumerate(firsts)]


def multiply(pairs, tiles, load, store):
    for start in range(0, len(pairs), BATCH):
        batch = pairs[start:start + BATCH]
        states = [jnp.concatenate([load(first), load(second)], axis=0) for _, first, second in batch]
        results = [product(tiles(i), x).astype(jnp.bfloat16) for (i, _, _), x in zip(batch, states)]
        for (_, first, second), y in zip(batch, results):
            rank = y.shape[0] // 2
            store(first, y[:rank])
            store(second, y[rank:])


def stack_tables(interp_ref, omega_ref, gains, turns, flips):
    rank = interp_ref.shape[-1]
    for table, out, scale in ((interp_ref, gains, 1.0), (omega_ref, turns, 0.5 / math.pi)):
        for flip in range(flips):
            for row in range(2):
                child = row ^ flip
                for column in range(2):
                    part = table[child, row ^ column].astype(jnp.float32) * scale
                    out[flip, row * rank:(row + 1) * rank, column * rank:(column + 1) * rank] = part


def scale_rows(warp_ref, rows):
    count = rows.shape[0]
    warp = jnp.broadcast_to(warp_ref[...].astype(jnp.float32), (count, count))
    diagonal = lax.broadcasted_iota(jnp.int32, (count, count), 0) == lax.broadcasted_iota(jnp.int32, (count, count), 1)
    column = jnp.sum(jnp.where(diagonal, warp, 0.0), axis=1, keepdims=True)
    rows[...] = jnp.broadcast_to(column, rows.shape)


def local_kernel(groups, group_bits, *refs):
    given, outs, rest = refs[:4], refs[4:4 + groups], refs[4 + groups:]
    warp_ref, interp_ref, omega_ref, state, gains, turns, rows, tiles, sems = rest
    copies = [pltpu.make_async_copy(src, dst, sems.at[i]) for i, (src, dst) in enumerate(zip(given, rest))]
    for copy in copies:
        copy.start()
    for copy in copies[:3]:
        copy.wait()
    stack_tables(interp_ref, omega_ref, gains, turns, 1)
    scale_rows(warp_ref, rows)
    total, rank, width = state.shape
    bits = total.bit_length() - 1
    place = lax.axis_index("src")

    def make_tiles(box):
        for child in range(2):
            half = slice(child * rank, (child + 1) * rank)
            wanted = [level for level in range(bits) if box >> level & 1 == child]
            if wanted:
                before, now = None, cosine(turns[0, half] * (rows[box:box + 1] * 0.25))
                twice = now + now
                for level in range(max(wanted) + 1):
                    if level:
                        before, now = now, twice * now - (1.0 if level == 1 else before)
                    if level in wanted:
                        low = box & ((1 << level) - 1)
                        tiles[level, ((box >> (level + 1)) << level) | low, half] = (gains[0, half] * now).astype(jnp.bfloat16)

    def load(box):
        return state[box]

    def store(box, y):
        state[box] = y

    def level_products(level, pairs):
        multiply(pairs, lambda i: tiles[level, i], load, store)

    size = 1 << group_bits
    for start in range(0, total + size, size):
        for box in range(start, min(start + size, total)):
            make_tiles(box)
        if start == 0:
            copies[3].wait()
        else:
            for level in range(group_bits):
                level_products(level, [p for p in pairs_of(total, level) if start - size <= p[1] < start])
    for level in range(group_bits, bits):
        level_products(level, pairs_of(total, level))

    part = total // groups
    warps = jnp.broadcast_to(warp_ref[...].astype(jnp.float32), (WARP_ROWS, total))
    warps = jnp.concatenate([warps, jnp.zeros((WARP_ROWS, width - total), jnp.float32)], axis=1).astype(jnp.bfloat16)
    for k in range(groups):
        outs[k][:part * rank] = state[pl.ds((place ^ k) * part, part)].reshape(part * rank, width)
        outs[k][part * rank:] = warps


def warp_rows(warps, place, part, rows):
    lanes = lax.broadcasted_iota(jnp.int32, warps.shape, 1)
    for m in range(part):
        column = jnp.sum(jnp.where(lanes == place * part + m, warps, 0.0), axis=1, keepdims=True)
        rows[m] = jnp.broadcast_to(column, rows.shape[1:])


def tiles_kernel(part, first_level, ks, warp_ref, interp_ref, omega_ref, tiles, last_tiles, gains, turns, rows):
    stack_tables(interp_ref, omega_ref, gains, turns, 2)
    rank = interp_ref.shape[-1]
    place, core = lax.axis_index("src"), lax.axis_index("tgt")
    warp_rows(warp_ref[...].astype(jnp.float32), place, part, rows)
    for j, k in enumerate(ks):
        for m in range(part):
            for step in range(tiles.shape[0]):
                side, s = place >> step & 1, k >> step & 1
                half = slice(s * rank, (s + 1) * rank)
                scale = rows[m, j:j + 1] * ((first_level + step + 1) / 4.0)
                tiles[step, k * part + m] = tile(gains[side, half], turns[side, half], scale)
            scale = rows[m, j:j + 1] * ((first_level + tiles.shape[0] + 1) / 4.0)
            last_tiles[k * part + m] = tile(gains[core, :rank], turns[core, :rank], scale)


def remote_kernel(groups, first_m, first_level, tiles, interp_ref, omega_ref, *rest):
    blocks, (out, gains, turns, rows) = rest[:groups], rest[groups:]
    stack_tables(interp_ref, omega_ref, gains, turns, 2)
    count, rank, width = out.shape
    some, part = count // groups, blocks[0].shape[0] // rank
    some_bits = some.bit_length() - 1
    place = lax.axis_index("src")
    warps = blocks[-1][part * rank:, :LANES].astype(jnp.float32)
    warp_rows(warps, place, part, rows)
    for step in range(groups.bit_length() - 1):
        side = place >> step & 1

        def half_tile(i, step=step, side=side):
            k, m = i // some, first_m + i % some
            if k < groups - 1:
                return tiles[step, k * part + m]
            scale = rows[m, :1] * ((first_level + step + 1) / 4.0)
            return tile(gains[side, rank:], turns[side, rank:], scale)

        def load(i, step=step):
            m = first_m + i % some
            return out[i] if step else blocks[i // some][m * rank:(m + 1) * rank]

        def store(i, y):
            out[i] = y

        def tile_of(i, step=step, half_tile=half_tile):
            first = split_pair(i, step + some_bits)
            return jnp.concatenate([half_tile(first), half_tile(first | (1 << (step + some_bits)))], axis=0)

        multiply(pairs_of(count, step + some_bits), tile_of, load, store)


def core_kernel(groups, halves, level, tiles, last_ref, interp_ref, omega_ref, *rest):
    own, other, rest = rest[:halves], rest[halves:2 * halves], rest[2 * halves:]
    outs, (gains, turns, rows) = rest[:groups], rest[groups:]
    stack_tables(interp_ref, omega_ref, gains, turns, 2)
    rank = interp_ref.shape[-1]
    some = own[0].shape[0] // groups
    part = some * halves
    place, core = lax.axis_index("src"), lax.axis_index("tgt")
    warp_rows(last_ref[part * rank:, :LANES].astype(jnp.float32), place, part, rows)
    for k in range(groups):
        for m in range(part):
            i = k * some + m % some
            x = jnp.concatenate([own[m // some][i], other[m // some][i]], axis=0)
            if k < groups - 1:
                tiles_m = tiles[k * part + m]
            else:
                tiles_m = tile(gains[core, :rank], turns[core, :rank], rows[m, :1] * ((level + 1) / 4.0))
            outs[k][m * rank:(m + 1) * rank] = product(tiles_m, x).astype(jnp.bfloat16)


def eval_kernel(ks, warp_ref, interp_ref, omega_ref, *rest):
    blocks = rest[:len(ks)]
    out_hbm, values, rows, sems = rest[-4:]
    rank = interp_ref.shape[-1]
    part = blocks[0].shape[0] // rank
    place = lax.axis_index("src")
    scale_rows(warp_ref, rows)
    gains = interp_ref[...].astype(jnp.float32)
    turns = omega_ref[...] * (0.5 / math.pi)
    gains, turns = jnp.concatenate([gains, gains], axis=1), jnp.concatenate([turns, turns], axis=1)
    left = lax.broadcasted_iota(jnp.int32, (1, 2 * rank), 1) < rank
    copies = []
    for n, k in enumerate(ks):
        group = place ^ k

        def scale_of(m):
            return rows[pl.ds(group * part + m, 1), :]

        for m in range(0, part, 2):
            if m + 1 < part:
                both = tile(gains, turns, jnp.where(left, scale_of(m), scale_of(m + 1)))
                none = jnp.zeros_like(both)
                tiles = jnp.concatenate([jnp.where(left, both, none), jnp.where(left, none, both)], axis=0)
                result = product(tiles, blocks[n][m * rank:(m + 2) * rank])
                values[n, m], values[n, m + 1] = result[:rank], result[rank:]
            else:
                tiles = tile(gains[:, :rank], turns[:, :rank], scale_of(m)[:, :rank])
                values[n, m] = product(tiles, blocks[n][m * rank:(m + 1) * rank])
        copy = pltpu.make_async_copy(values.at[n], out_hbm.at[group], sems.at[n])
        copy.start()
        copies.append(copy)
    for copy in copies:
        copy.wait()


def on_device(sources, warp, interp, omega, eval_interp, eval_omega):
    total, rank, width = sources.shape
    bits = total.bit_length() - 1
    groups = lax.axis_size("src")
    group_bits = groups.bit_length() - 1
    part = total // groups
    halves = min(HALVES, part)
    bf16, f32 = jnp.bfloat16, jnp.float32
    params = pltpu.CompilerParams(vmem_limit_bytes=VMEM_LIMIT)
    warp = warp.reshape(1, total)
    block = jax.ShapeDtypeStruct((part * rank, width), bf16)
    long_block = jax.ShapeDtypeStruct((part * rank + WARP_ROWS, width), bf16)
    both_tables = [pltpu.VMEM((2, 2 * rank, 2 * rank), f32)] * 2
    far, near = list(range(groups // 2, groups)), list(range(1, groups // 2))
    order = [k for pair in zip(far, near) for k in pair] + far[len(near):]

    def cost(steps):
        return pl.CostEstimate(flops=steps, bytes_accessed=steps, transcendentals=0)

    def after(value, done):
        return lax.optimization_barrier((value, done))[0]

    def moved(value, k):
        return lax.ppermute(value, "src", [(i, i ^ k) for i in range(groups)])

    blocks = pl.pallas_call(
        functools.partial(local_kernel, groups, min(GROUP_BITS, bits)),
        out_shape=[long_block] * groups,
        in_specs=[HBM] * 4,
        out_specs=[VMEM] * groups,
        scratch_shapes=[
            pltpu.VMEM(warp.shape, warp.dtype),
            pltpu.VMEM(interp.shape, interp.dtype),
            pltpu.VMEM(omega.shape, omega.dtype),
            pltpu.VMEM((total, rank, width), bf16),
            pltpu.VMEM((1, 2 * rank, 2 * rank), f32),
            pltpu.VMEM((1, 2 * rank, 2 * rank), f32),
            pltpu.VMEM((total, LANES), f32),
            pltpu.VMEM((bits, total // 2, 2 * rank, 2 * rank), bf16),
            pltpu.SemaphoreType.DMA((4,)),
        ],
        compiler_params=params,
        cost_estimate=cost(total // 2 * bits),
        name="local",
    )(warp, interp, omega, sources)
    arrived = {0: blocks[0]}
    for k in order:
        arrived[k] = moved(blocks[k], k)
    known = [0] + order[:-1]
    all_warp = jnp.concatenate([arrived[k][part * rank:part * rank + 1, :total] for k in known], axis=0)
    tiles, last_tiles = pl.pallas_call(
        functools.partial(tiles_kernel, part, bits, known),
        out_shape=[
            jax.ShapeDtypeStruct((group_bits, total - part, rank, 2 * rank), bf16),
            jax.ShapeDtypeStruct((total - part, rank, 2 * rank), bf16),
        ],
        in_specs=[VMEM, VMEM, VMEM],
        out_specs=[VMEM, VMEM],
        scratch_shapes=both_tables + [pltpu.VMEM((part, groups - 1, LANES), f32)],
        compiler_params=params,
        cost_estimate=cost(total // 2 * (group_bits + 1)),
        name="remote_tiles",
    )(all_warp, interp, omega)
    last_rows = pltpu.VMEM((part, WARP_ROWS, LANES), f32)
    last_block = arrived[groups - 1]
    states = []
    for half in range(halves):
        first_m = half * (part // halves)
        by_k = [arrived[k] for k in range(groups)]
        if half:
            by_k[0] = after(by_k[0], states[0])
        states.append(pl.pallas_call(
            functools.partial(remote_kernel, groups, first_m, bits),
            out_shape=jax.ShapeDtypeStruct((total // halves, rank, width), bf16),
            in_specs=[VMEM] * (3 + groups),
            out_specs=VMEM,
            scratch_shapes=both_tables + [last_rows],
            compiler_params=params,
            cost_estimate=cost(total // 2 // halves * group_bits),
            name=f"remote_{half}",
        )(tiles, interp, omega, *by_k))
    others = [lax.ppermute(state, "tgt", [(i, i ^ 1) for i in range(lax.axis_size("tgt"))]) for state in states]
    blocks = pl.pallas_call(
        functools.partial(core_kernel, groups, halves, bits + group_bits),
        out_shape=[block] * groups,
        in_specs=[VMEM] * (4 + 2 * halves),
        out_specs=[VMEM] * groups,
        scratch_shapes=both_tables + [last_rows],
        compiler_params=params,
        cost_estimate=cost(total // 2),
        name="core",
    )(last_tiles, last_block, interp, omega, *states, *others)
    arrived = {0: blocks[0]}
    for k in order:
        arrived[k] = moved(blocks[k], k)
    early = [0] + order[:len(order) // 2]
    values = None
    for name, ks in (("early", early), ("late", [k for k in order if k not in early])):
        operands = [warp, eval_interp, eval_omega] + [arrived[k] for k in ks]
        specs = [VMEM] * len(operands)
        aliases = {}
        if values is not None:
            aliases = {len(operands): 0}
            operands.append(values)
            specs.append(ANY)
        values = pl.pallas_call(
            functools.partial(eval_kernel, ks),
            out_shape=jax.ShapeDtypeStruct((groups, part, rank, width), f32),
            in_specs=specs,
            out_specs=ANY,
            scratch_shapes=[
                pltpu.VMEM((len(ks), part, rank, width), f32),
                pltpu.VMEM((total, LANES), f32),
                pltpu.SemaphoreType.DMA((len(ks),)),
            ],
            input_output_aliases=aliases,
            compiler_params=params,
            cost_estimate=cost(len(ks) * part // 2),
            name=f"eval_{name}",
        )(*operands)
    return values.reshape(total, rank, width)


def solution(mesh):
    in_specs = (P(("grp", "src", "tgt"), None, None), P(("grp", "src", "tgt")), P(), P(), P(), P())
    out_specs = P(("grp", "src", "tgt"), None, None)
    return jax.shard_map(
        on_device, mesh=mesh, in_specs=in_specs, out_specs=out_specs, check_vma=False
    )
```

```python
import functools
import math

import jax
import jax.numpy as jnp
from jax import lax
from jax.experimental import pallas as pl
from jax.experimental.pallas import tpu as pltpu
from jax.sharding import PartitionSpec as P

KNOWN = 4
BATCH = 16
GROUP_BITS = 3
HALVES = 2
VMEM_LIMIT = 20 * 1024 * 1024
LOCAL_VMEM_LIMIT = 60 * 1024 * 1024
WARP_ROWS = 16
VMEM = pl.BlockSpec(memory_space=pltpu.VMEM)
ANY = pl.BlockSpec(memory_space=pl.ANY)
HBM = pl.BlockSpec(memory_space=pltpu.HBM)
SINE = (6.28318516, -41.34165503, 81.60100405, -76.54978181, 39.53670223)
LANES = 128


def cosine(turns):
    u = turns - jnp.round(turns)
    z = 0.25 - jnp.abs(u)
    v = z * z
    poly = SINE[-1]
    for coefficient in SINE[-2::-1]:
        poly = poly * v + coefficient
    return z * poly


def tile(gains, turns, scale):
    return (gains * cosine(turns * scale)).astype(jnp.bfloat16)


def product(tiles, state):
    return jnp.dot(tiles, state, preferred_element_type=jnp.float32)


def split_pair(index, bit):
    low = index & ((1 << bit) - 1)
    return ((index >> bit) << (bit + 1)) | low


def pairs_of(count, bit):
    firsts = [split_pair(i, bit) for i in range(count // 2)]
    return [(i, first, first | (1 << bit)) for i, first in enumerate(firsts)]


def multiply(pairs, tiles, load, store):
    for start in range(0, len(pairs), BATCH):
        batch = pairs[start:start + BATCH]
        states = [jnp.concatenate([load(first), load(second)], axis=0) for _, first, second in batch]
        results = [product(tiles(i), x).astype(jnp.bfloat16) for (i, _, _), x in zip(batch, states)]
        for (_, first, second), y in zip(batch, results):
            rank = y.shape[0] // 2
            store(first, y[:rank])
            store(second, y[rank:])


def stack_tables(interp_ref, omega_ref, gains, turns, flips):
    rank = interp_ref.shape[-1]
    for table, out, scale in ((interp_ref, gains, 1.0), (omega_ref, turns, 0.5 / math.pi)):
        for flip in range(flips):
            for row in range(2):
                child = row ^ flip
                for column in range(2):
                    part = table[child, row ^ column].astype(jnp.float32) * scale
                    out[flip, row * rank:(row + 1) * rank, column * rank:(column + 1) * rank] = part


def scale_rows(warp_ref, rows):
    count = rows.shape[0]
    warp = jnp.broadcast_to(warp_ref[...].astype(jnp.float32), (count, count))
    diagonal = lax.broadcasted_iota(jnp.int32, (count, count), 0) == lax.broadcasted_iota(jnp.int32, (count, count), 1)
    column = jnp.sum(jnp.where(diagonal, warp, 0.0), axis=1, keepdims=True)
    rows[...] = jnp.broadcast_to(column, rows.shape)


def local_kernel(groups, halves, group_bits, *refs):
    given, outs, rest = refs[:4], refs[4:4 + halves * groups], refs[4 + halves * groups:]
    warp_ref, interp_ref, omega_ref, state, gains, turns, rows, tiles, sems = rest
    copies = [pltpu.make_async_copy(src, dst, sems.at[i]) for i, (src, dst) in enumerate(zip(given, rest))]
    for copy in copies:
        copy.start()
    for copy in copies[:3]:
        copy.wait()
    stack_tables(interp_ref, omega_ref, gains, turns, 1)
    scale_rows(warp_ref, rows)
    total, rank, width = state.shape
    bits = total.bit_length() - 1
    place = lax.axis_index("src")

    def make_tiles(box):
        for child in range(2):
            half = slice(child * rank, (child + 1) * rank)
            wanted = [level for level in range(bits) if box >> level & 1 == child]
            if wanted:
                before, now = None, cosine(turns[0, half] * (rows[box:box + 1] * 0.25))
                twice = now + now
                for level in range(max(wanted) + 1):
                    if level:
                        before, now = now, twice * now - (1.0 if level == 1 else before)
                    if level in wanted:
                        low = box & ((1 << level) - 1)
                        tiles[level, ((box >> (level + 1)) << level) | low, half] = (gains[0, half] * now).astype(jnp.bfloat16)

    def load(box):
        return state[box]

    def store(box, y):
        state[box] = y

    def level_products(level, pairs):
        multiply(pairs, lambda i: tiles[level, i], load, store)

    size = 1 << group_bits
    for start in range(0, total + size, size):
        for box in range(start, min(start + size, total)):
            make_tiles(box)
        if start == 0:
            copies[3].wait()
        else:
            for level in range(group_bits):
                level_products(level, [p for p in pairs_of(total, level) if start - size <= p[1] < start])
    for level in range(group_bits, bits):
        level_products(level, pairs_of(total, level))

    part = total // groups
    warps = jnp.broadcast_to(warp_ref[...].astype(jnp.float32), (WARP_ROWS, total))
    warps = jnp.concatenate([warps, jnp.zeros((WARP_ROWS, width - total), jnp.float32)], axis=1).astype(jnp.bfloat16)
    some = part // halves
    for k in range(groups):
        for half in range(halves):
            out = outs[half * groups + k]
            out[:some * rank] = state[pl.ds((place ^ k) * part + half * some, some)].reshape(some * rank, width)
            if half == 0:
                out[some * rank:] = warps


def warp_rows(warps, place, part, rows):
    lanes = lax.broadcasted_iota(jnp.int32, warps.shape, 1)
    for m in range(part):
        column = jnp.sum(jnp.where(lanes == place * part + m, warps, 0.0), axis=1, keepdims=True)
        rows[m] = jnp.broadcast_to(column, rows.shape[1:])


def tiles_kernel(part, first_level, ks, warp_ref, interp_ref, omega_ref, tiles, last_tiles, gains, turns, rows):
    stack_tables(interp_ref, omega_ref, gains, turns, 2)
    rank = interp_ref.shape[-1]
    place, core = lax.axis_index("src"), lax.axis_index("tgt")
    warp_rows(warp_ref[...].astype(jnp.float32), place, part, rows)
    for j, k in enumerate(ks):
        for m in range(part):
            for step in range(tiles.shape[0]):
                side, s = place >> step & 1, k >> step & 1
                half = slice(s * rank, (s + 1) * rank)
                scale = rows[m, j:j + 1] * ((first_level + step + 1) / 4.0)
                tiles[step, j * part + m] = tile(gains[side, half], turns[side, half], scale)
            scale = rows[m, j:j + 1] * ((first_level + tiles.shape[0] + 1) / 4.0)
            last_tiles[j * part + m] = tile(gains[core, :rank], turns[core, :rank], scale)


def remote_kernel(groups, first_m, part, first_level, known, tiles, interp_ref, omega_ref, *rest):
    unknown = [k for k in range(groups) if k not in known]
    blocks, late, (out, gains, turns, rows) = rest[:groups], rest[groups:groups + len(unknown)], rest[groups + len(unknown):]
    stack_tables(interp_ref, omega_ref, gains, turns, 2)
    count, rank, width = out.shape
    some = count // groups
    some_bits = some.bit_length() - 1
    place = lax.axis_index("src")
    for j, ref in enumerate(late):
        warp_rows(ref[ref.shape[0] - WARP_ROWS:, :LANES].astype(jnp.float32), place, part, rows.at[j])
    for step in range(groups.bit_length() - 1):
        side = place >> step & 1

        def half_tile(i, step=step, side=side):
            k, m = i // some, first_m + i % some
            if k in known:
                return tiles[step, known.index(k) * part + m]
            scale = rows[unknown.index(k), m, :1] * ((first_level + step + 1) / 4.0)
            half = slice((k >> step & 1) * rank, ((k >> step & 1) + 1) * rank)
            return tile(gains[side, half], turns[side, half], scale)

        def load(i, step=step):
            m = i % some
            return out[i] if step else blocks[i // some][m * rank:(m + 1) * rank]

        def store(i, y):
            out[i] = y

        def tile_of(i, step=step, half_tile=half_tile):
            first = split_pair(i, step + some_bits)
            return jnp.concatenate([half_tile(first), half_tile(first | (1 << (step + some_bits)))], axis=0)

        multiply(pairs_of(count, step + some_bits), tile_of, load, store)


def core_kernel(groups, first_m, part, level, known, tiles, interp_ref, omega_ref, own, other, *rest):
    unknown = [k for k in range(groups) if k not in known]
    late, rest = rest[:len(unknown)], rest[len(unknown):]
    outs, (gains, turns, rows) = rest[:groups], rest[groups:]
    stack_tables(interp_ref, omega_ref, gains, turns, 2)
    rank = interp_ref.shape[-1]
    some = own.shape[0] // groups
    place, core = lax.axis_index("src"), lax.axis_index("tgt")
    for j, ref in enumerate(late):
        warp_rows(ref[ref.shape[0] - WARP_ROWS:, :LANES].astype(jnp.float32), place, part, rows.at[j])
    for k in range(groups):
        for m in range(some):
            x = jnp.concatenate([own[k * some + m], other[k * some + m]], axis=0)
            if k in known:
                tiles_m = tiles[known.index(k) * part + first_m + m]
            else:
                scale = rows[unknown.index(k), first_m + m, :1] * ((level + 1) / 4.0)
                tiles_m = tile(gains[core, :rank], turns[core, :rank], scale)
            outs[k][m * rank:(m + 1) * rank] = product(tiles_m, x).astype(jnp.bfloat16)


def eval_kernel(part, items, warp_ref, interp_ref, omega_ref, *rest):
    blocks = rest[:len(items)]
    out_hbm, values, rows, sems = rest[-4:]
    rank = interp_ref.shape[-1]
    some = blocks[0].shape[0] // rank
    place = lax.axis_index("src")
    scale_rows(warp_ref, rows)
    gains = interp_ref[...].astype(jnp.float32)
    turns = omega_ref[...] * (0.5 / math.pi)
    gains, turns = jnp.concatenate([gains, gains], axis=1), jnp.concatenate([turns, turns], axis=1)
    left = lax.broadcasted_iota(jnp.int32, (1, 2 * rank), 1) < rank
    copies = []
    for n, (k, first) in enumerate(items):
        group = place ^ k

        def scale_of(m):
            return rows[pl.ds(group * part + first + m, 1), :]

        for m in range(0, some, 2):
            if m + 1 < some:
                both = tile(gains, turns, jnp.where(left, scale_of(m), scale_of(m + 1)))
                none = jnp.zeros_like(both)
                tiles = jnp.concatenate([jnp.where(left, both, none), jnp.where(left, none, both)], axis=0)
                result = product(tiles, blocks[n][m * rank:(m + 2) * rank])
                values[n, m], values[n, m + 1] = result[:rank], result[rank:]
            else:
                tiles = tile(gains[:, :rank], turns[:, :rank], scale_of(m)[:, :rank])
                values[n, m] = product(tiles, blocks[n][m * rank:(m + 1) * rank])
        copy = pltpu.make_async_copy(values.at[n], out_hbm.at[group, first:first + some], sems.at[n])
        copy.start()
        copies.append(copy)
    for copy in copies:
        copy.wait()


def on_device(sources, warp, interp, omega, eval_interp, eval_omega):
    total, rank, width = sources.shape
    bits = total.bit_length() - 1
    groups = lax.axis_size("src")
    group_bits = groups.bit_length() - 1
    part = total // groups
    halves = min(HALVES, part)
    some = part // halves
    bf16, f32 = jnp.bfloat16, jnp.float32
    params = pltpu.CompilerParams(vmem_limit_bytes=VMEM_LIMIT)
    warp = warp.reshape(1, total)
    block = jax.ShapeDtypeStruct((some * rank, width), bf16)
    long_block = jax.ShapeDtypeStruct((some * rank + WARP_ROWS, width), bf16)
    both_tables = [pltpu.VMEM((2, 2 * rank, 2 * rank), f32)] * 2
    far, near = list(range(groups // 2, groups)), list(range(1, groups // 2))
    order = [k for pair in zip(far, near) for k in pair] + far[len(near):]

    def cost(steps):
        return pl.CostEstimate(flops=steps, bytes_accessed=steps, transcendentals=0)

    def after(value, done):
        return lax.optimization_barrier((value, done))[0]

    def moved(value, k):
        return lax.ppermute(value, "src", [(i, i ^ k) for i in range(groups)])

    blocks = pl.pallas_call(
        functools.partial(local_kernel, groups, halves, min(GROUP_BITS, bits)),
        out_shape=[long_block] * groups + [block] * ((halves - 1) * groups),
        in_specs=[HBM] * 4,
        out_specs=[VMEM] * (halves * groups),
        scratch_shapes=[
            pltpu.VMEM(warp.shape, warp.dtype),
            pltpu.VMEM(interp.shape, interp.dtype),
            pltpu.VMEM(omega.shape, omega.dtype),
            pltpu.VMEM((total, rank, width), bf16),
            pltpu.VMEM((1, 2 * rank, 2 * rank), f32),
            pltpu.VMEM((1, 2 * rank, 2 * rank), f32),
            pltpu.VMEM((total, LANES), f32),
            pltpu.VMEM((bits, total // 2, 2 * rank, 2 * rank), bf16),
            pltpu.SemaphoreType.DMA((4,)),
        ],
        compiler_params=pltpu.CompilerParams(vmem_limit_bytes=LOCAL_VMEM_LIMIT),
        cost_estimate=cost(total // 2 * bits),
        name="local",
    )(warp, interp, omega, sources)
    def exchanged(blocks):
        arrived = {0: blocks[0]}
        for k in order:
            arrived[k] = moved(blocks[k], k)
        return arrived

    arrived = [exchanged(blocks[half * groups:(half + 1) * groups]) for half in range(halves)]
    known = [0] + order[:KNOWN] if groups > KNOWN + 1 else list(range(groups - 1))
    all_warp = jnp.concatenate([arrived[0][k][some * rank:some * rank + 1, :total] for k in known], axis=0)
    tiles, last_tiles = pl.pallas_call(
        functools.partial(tiles_kernel, part, bits, known),
        out_shape=[
            jax.ShapeDtypeStruct((group_bits, len(known) * part, rank, 2 * rank), bf16),
            jax.ShapeDtypeStruct((len(known) * part, rank, 2 * rank), bf16),
        ],
        in_specs=[VMEM, VMEM, VMEM],
        out_specs=[VMEM, VMEM],
        scratch_shapes=both_tables + [pltpu.VMEM((part, len(known), LANES), f32)],
        compiler_params=params,
        cost_estimate=cost(total // 2 * (group_bits + 1)),
        name="remote_tiles",
    )(all_warp, interp, omega)
    late_rows = pltpu.VMEM((groups - len(known), part, WARP_ROWS, LANES), f32)
    late = [arrived[0][k] for k in range(groups) if k not in known]
    returned = []
    for half in range(halves):
        state = pl.pallas_call(
            functools.partial(remote_kernel, groups, half * some, part, bits, known),
            out_shape=jax.ShapeDtypeStruct((groups * some, rank, width), bf16),
            in_specs=[VMEM] * (3 + groups + len(late)),
            out_specs=VMEM,
            scratch_shapes=both_tables + [late_rows],
            compiler_params=params,
            cost_estimate=cost(total // 2 // halves * group_bits),
            name=f"remote_{half}",
        )(tiles, interp, omega, *[arrived[half][k] for k in range(groups)], *late)
        other = lax.ppermute(state, "tgt", [(i, i ^ 1) for i in range(lax.axis_size("tgt"))])
        blocks = pl.pallas_call(
            functools.partial(core_kernel, groups, half * some, part, bits + group_bits, known),
            out_shape=[block] * groups,
            in_specs=[VMEM] * (5 + len(late)),
            out_specs=[VMEM] * groups,
            scratch_shapes=both_tables + [late_rows],
            compiler_params=params,
            cost_estimate=cost(total // 2 // halves),
            name=f"core_{half}",
        )(last_tiles, interp, omega, state, other, *late)
        returned.append(exchanged(blocks))
    values = None
    items = [(k, half) for half in range(halves) for k in [0] + order]
    cuts = [0, len(items) // 2, len(items) - len(order) // 2, len(items)]
    for i, (start, stop) in enumerate(zip(cuts, cuts[1:])):
        chosen = items[start:stop]
        operands = [warp, eval_interp, eval_omega] + [returned[half][k] for k, half in chosen]
        specs = [VMEM] * len(operands)
        aliases = {}
        if values is not None:
            aliases = {len(operands): 0}
            operands.append(values)
            specs.append(ANY)
        values = pl.pallas_call(
            functools.partial(eval_kernel, part, [(k, half * some) for k, half in chosen]),
            out_shape=jax.ShapeDtypeStruct((groups, part, rank, width), f32),
            in_specs=specs,
            out_specs=ANY,
            scratch_shapes=[
                pltpu.VMEM((len(chosen), some, rank, width), f32),
                pltpu.VMEM((total, LANES), f32),
                pltpu.SemaphoreType.DMA((len(chosen),)),
            ],
            input_output_aliases=aliases,
            compiler_params=params,
            cost_estimate=cost(len(chosen)),
            name=f"eval_{i}",
        )(*operands)
    return values.reshape(total, rank, width)


def solution(mesh):
    in_specs = (P(("grp", "src", "tgt"), None, None), P(("grp", "src", "tgt")), P(), P(), P(), P())
    out_specs = P(("grp", "src", "tgt"), None, None)
    return jax.shard_map(
        on_device, mesh=mesh, in_specs=in_specs, out_specs=out_specs, check_vma=False
    )
```

```python
import functools
import math

import jax
import jax.numpy as jnp
from jax import lax
from jax.experimental import pallas as pl
from jax.experimental.pallas import tpu as pltpu
from jax.sharding import PartitionSpec as P

KNOWN = 4
BATCH = 16
GROUP_BITS = 3
HALVES = 2
VMEM_LIMIT = 20 * 1024 * 1024
LOCAL_VMEM_LIMIT = 60 * 1024 * 1024
WARP_ROWS = 16
VMEM = pl.BlockSpec(memory_space=pltpu.VMEM)
ANY = pl.BlockSpec(memory_space=pl.ANY)
HBM = pl.BlockSpec(memory_space=pltpu.HBM)
SINE = (6.28318516, -41.34165503, 81.60100405, -76.54978181, 39.53670223)
LANES = 128


def cosine(turns):
    u = turns - jnp.round(turns)
    z = 0.25 - jnp.abs(u)
    v = z * z
    poly = SINE[-1]
    for coefficient in SINE[-2::-1]:
        poly = poly * v + coefficient
    return z * poly


def tile(gains, turns, scale):
    return (gains * cosine(turns * scale)).astype(jnp.bfloat16)


def product(tiles, state):
    return jnp.dot(tiles, state, preferred_element_type=jnp.float32)


def split_pair(index, bit):
    low = index & ((1 << bit) - 1)
    return ((index >> bit) << (bit + 1)) | low


def pairs_of(count, bit):
    firsts = [split_pair(i, bit) for i in range(count // 2)]
    return [(i, first, first | (1 << bit)) for i, first in enumerate(firsts)]


def multiply(pairs, tiles, load, store):
    for start in range(0, len(pairs), BATCH):
        batch = pairs[start:start + BATCH]
        states = [jnp.concatenate([load(first), load(second)], axis=0) for _, first, second in batch]
        results = [product(tiles(i), x).astype(jnp.bfloat16) for (i, _, _), x in zip(batch, states)]
        for (_, first, second), y in zip(batch, results):
            rank = y.shape[0] // 2
            store(first, y[:rank])
            store(second, y[rank:])


def stack_tables(interp_ref, omega_ref, gains, turns, flips):
    rank = interp_ref.shape[-1]
    for table, out, scale in ((interp_ref, gains, 1.0), (omega_ref, turns, 0.5 / math.pi)):
        for flip in range(flips):
            for row in range(2):
                child = row ^ flip
                for column in range(2):
                    part = table[child, row ^ column].astype(jnp.float32) * scale
                    out[flip, row * rank:(row + 1) * rank, column * rank:(column + 1) * rank] = part


def scale_rows(warp_ref, rows):
    count = rows.shape[0]
    warp = jnp.broadcast_to(warp_ref[...].astype(jnp.float32), (count, count))
    diagonal = lax.broadcasted_iota(jnp.int32, (count, count), 0) == lax.broadcasted_iota(jnp.int32, (count, count), 1)
    column = jnp.sum(jnp.where(diagonal, warp, 0.0), axis=1, keepdims=True)
    rows[...] = jnp.broadcast_to(column, rows.shape)


def local_kernel(groups, halves, group_bits, *refs):
    given, outs, rest = refs[:4], refs[4:4 + halves * groups], refs[4 + halves * groups:]
    warp_ref, interp_ref, omega_ref, state, gains, turns, rows, tiles, sems = rest
    copies = [pltpu.make_async_copy(src, dst, sems.at[i]) for i, (src, dst) in enumerate(zip(given, rest))]
    for copy in copies:
        copy.start()
    for copy in copies[:3]:
        copy.wait()
    stack_tables(interp_ref, omega_ref, gains, turns, 1)
    scale_rows(warp_ref, rows)
    total, rank, width = state.shape
    bits = total.bit_length() - 1
    place = lax.axis_index("src")

    def make_tiles(box):
        for child in range(2):
            half = slice(child * rank, (child + 1) * rank)
            wanted = [level for level in range(bits) if box >> level & 1 == child]
            if wanted:
                before, now = None, cosine(turns[0, half] * (rows[box:box + 1] * 0.25))
                twice = now + now
                for level in range(max(wanted) + 1):
                    if level:
                        before, now = now, twice * now - (1.0 if level == 1 else before)
                    if level in wanted:
                        low = box & ((1 << level) - 1)
                        tiles[level, ((box >> (level + 1)) << level) | low, half] = (gains[0, half] * now).astype(jnp.bfloat16)

    def load(box):
        return state[box]

    def store(box, y):
        state[box] = y

    def level_products(level, pairs):
        multiply(pairs, lambda i: tiles[level, i], load, store)

    size = 1 << group_bits
    for start in range(0, total + size, size):
        for box in range(start, min(start + size, total)):
            make_tiles(box)
        if start == 0:
            copies[3].wait()
        else:
            for level in range(group_bits):
                level_products(level, [p for p in pairs_of(total, level) if start - size <= p[1] < start])
    for level in range(group_bits, bits):
        level_products(level, pairs_of(total, level))

    part = total // groups
    warps = jnp.broadcast_to(warp_ref[...].astype(jnp.float32), (WARP_ROWS, total))
    warps = jnp.concatenate([warps, jnp.zeros((WARP_ROWS, width - total), jnp.float32)], axis=1).astype(jnp.bfloat16)
    some = part // halves
    for k in range(groups):
        for half in range(halves):
            out = outs[half * groups + k]
            out[:some * rank] = state[pl.ds((place ^ k) * part + half * some, some)].reshape(some * rank, width)
            if half == 0:
                out[some * rank:] = warps


def warp_rows(warps, place, part, rows):
    lanes = lax.broadcasted_iota(jnp.int32, warps.shape, 1)
    for m in range(part):
        column = jnp.sum(jnp.where(lanes == place * part + m, warps, 0.0), axis=1, keepdims=True)
        rows[m] = jnp.broadcast_to(column, rows.shape[1:])


def tiles_kernel(part, first_level, ks, warp_ref, interp_ref, omega_ref, tiles, last_tiles, gains, turns, rows):
    stack_tables(interp_ref, omega_ref, gains, turns, 2)
    rank = interp_ref.shape[-1]
    place, core = lax.axis_index("src"), lax.axis_index("tgt")
    warp_rows(warp_ref[...].astype(jnp.float32), place, part, rows)
    for j, k in enumerate(ks):
        for m in range(part):
            for step in range(tiles.shape[0]):
                side, s = place >> step & 1, k >> step & 1
                half = slice(s * rank, (s + 1) * rank)
                scale = rows[m, j:j + 1] * ((first_level + step + 1) / 4.0)
                tiles[step, j * part + m] = tile(gains[side, half], turns[side, half], scale)
            scale = rows[m, j:j + 1] * ((first_level + tiles.shape[0] + 1) / 4.0)
            last_tiles[j * part + m] = tile(gains[core, :rank], turns[core, :rank], scale)


def remote_kernel(groups, first_m, part, first_level, known, tiles, interp_ref, omega_ref, *rest):
    unknown = [k for k in range(groups) if k not in known]
    blocks, late, (out, gains, turns, rows) = rest[:groups], rest[groups:groups + len(unknown)], rest[groups + len(unknown):]
    stack_tables(interp_ref, omega_ref, gains, turns, 2)
    count, rank, width = out.shape
    some = count // groups
    some_bits = some.bit_length() - 1
    place = lax.axis_index("src")
    for j, ref in enumerate(late):
        warp_rows(ref[ref.shape[0] - WARP_ROWS:, :LANES].astype(jnp.float32), place, part, rows.at[j])
    for step in range(groups.bit_length() - 1):
        side = place >> step & 1

        def half_tile(i, step=step, side=side):
            k, m = i // some, first_m + i % some
            if k in known:
                return tiles[step, known.index(k) * part + m]
            scale = rows[unknown.index(k), m, :1] * ((first_level + step + 1) / 4.0)
            half = slice((k >> step & 1) * rank, ((k >> step & 1) + 1) * rank)
            return tile(gains[side, half], turns[side, half], scale)

        def load(i, step=step):
            m = i % some
            return out[i] if step else blocks[i // some][m * rank:(m + 1) * rank]

        def store(i, y):
            out[i] = y

        def tile_of(i, step=step, half_tile=half_tile):
            first = split_pair(i, step + some_bits)
            return jnp.concatenate([half_tile(first), half_tile(first | (1 << (step + some_bits)))], axis=0)

        multiply(pairs_of(count, step + some_bits), tile_of, load, store)


def core_kernel(groups, first_m, part, level, known, tiles, interp_ref, omega_ref, own, other, *rest):
    unknown = [k for k in range(groups) if k not in known]
    late, rest = rest[:len(unknown)], rest[len(unknown):]
    outs, (gains, turns, rows) = rest[:groups], rest[groups:]
    stack_tables(interp_ref, omega_ref, gains, turns, 2)
    rank = interp_ref.shape[-1]
    some = own.shape[0] // groups
    place, core = lax.axis_index("src"), lax.axis_index("tgt")
    for j, ref in enumerate(late):
        warp_rows(ref[ref.shape[0] - WARP_ROWS:, :LANES].astype(jnp.float32), place, part, rows.at[j])
    for k in range(groups):
        for m in range(some):
            x = jnp.concatenate([own[k * some + m], other[k * some + m]], axis=0)
            if k in known:
                tiles_m = tiles[known.index(k) * part + first_m + m]
            else:
                scale = rows[unknown.index(k), first_m + m, :1] * ((level + 1) / 4.0)
                tiles_m = tile(gains[core, :rank], turns[core, :rank], scale)
            outs[k][m * rank:(m + 1) * rank] = product(tiles_m, x).astype(jnp.bfloat16)


def eval_kernel(part, items, warp_ref, interp_ref, omega_ref, *rest):
    blocks = rest[:len(items)]
    out_hbm, values, rows, sems = rest[-4:]
    rank = interp_ref.shape[-1]
    some = blocks[0].shape[0] // rank
    place = lax.axis_index("src")
    scale_rows(warp_ref, rows)
    gains = interp_ref[...].astype(jnp.float32)
    turns = omega_ref[...] * (0.5 / math.pi)
    gains, turns = jnp.concatenate([gains, gains], axis=1), jnp.concatenate([turns, turns], axis=1)
    left = lax.broadcasted_iota(jnp.int32, (1, 2 * rank), 1) < rank
    copies = []
    for n, (k, first) in enumerate(items):
        group = place ^ k

        def scale_of(m):
            return rows[pl.ds(group * part + first + m, 1), :]

        for m in range(0, some, 2):
            if m + 1 < some:
                both = tile(gains, turns, jnp.where(left, scale_of(m), scale_of(m + 1)))
                none = jnp.zeros_like(both)
                tiles = jnp.concatenate([jnp.where(left, both, none), jnp.where(left, none, both)], axis=0)
                result = product(tiles, blocks[n][m * rank:(m + 2) * rank])
                values[n, m], values[n, m + 1] = result[:rank], result[rank:]
            else:
                tiles = tile(gains[:, :rank], turns[:, :rank], scale_of(m)[:, :rank])
                values[n, m] = product(tiles, blocks[n][m * rank:(m + 1) * rank])
        copy = pltpu.make_async_copy(values.at[n], out_hbm.at[group, first:first + some], sems.at[n])
        copy.start()
        copies.append(copy)
    for copy in copies:
        copy.wait()


def on_device(sources, warp, interp, omega, eval_interp, eval_omega):
    total, rank, width = sources.shape
    bits = total.bit_length() - 1
    groups = lax.axis_size("src")
    group_bits = groups.bit_length() - 1
    part = total // groups
    halves = min(HALVES, part)
    some = part // halves
    bf16, f32 = jnp.bfloat16, jnp.float32
    params = pltpu.CompilerParams(vmem_limit_bytes=VMEM_LIMIT)
    warp = warp.reshape(1, total)
    block = jax.ShapeDtypeStruct((some * rank, width), bf16)
    long_block = jax.ShapeDtypeStruct((some * rank + WARP_ROWS, width), bf16)
    both_tables = [pltpu.VMEM((2, 2 * rank, 2 * rank), f32)] * 2
    far, near = list(range(groups // 2, groups)), list(range(1, groups // 2))
    far_order, near_order = sorted(far, key=lambda k: (k & 1, -k)), sorted(near, key=lambda k: (k & 1, k))
    order = [k for pair in zip(far_order, near_order) for k in pair] + far_order[len(near):]

    def cost(steps):
        return pl.CostEstimate(flops=steps, bytes_accessed=steps, transcendentals=0)

    def after(value, done):
        return lax.optimization_barrier((value, done))[0]

    def moved(value, k):
        return lax.ppermute(value, "src", [(i, i ^ k) for i in range(groups)])

    blocks = pl.pallas_call(
        functools.partial(local_kernel, groups, halves, min(GROUP_BITS, bits)),
        out_shape=[long_block] * groups + [block] * ((halves - 1) * groups),
        in_specs=[HBM] * 4,
        out_specs=[VMEM] * (halves * groups),
        scratch_shapes=[
            pltpu.VMEM(warp.shape, warp.dtype),
            pltpu.VMEM(interp.shape, interp.dtype),
            pltpu.VMEM(omega.shape, omega.dtype),
            pltpu.VMEM((total, rank, width), bf16),
            pltpu.VMEM((1, 2 * rank, 2 * rank), f32),
            pltpu.VMEM((1, 2 * rank, 2 * rank), f32),
            pltpu.VMEM((total, LANES), f32),
            pltpu.VMEM((bits, total // 2, 2 * rank, 2 * rank), bf16),
            pltpu.SemaphoreType.DMA((4,)),
        ],
        compiler_params=pltpu.CompilerParams(vmem_limit_bytes=LOCAL_VMEM_LIMIT),
        cost_estimate=cost(total // 2 * bits),
        name="local",
    )(warp, interp, omega, sources)
    def exchanged(blocks):
        arrived = {0: blocks[0]}
        for k in order:
            arrived[k] = moved(blocks[k], k)
        return arrived

    arrived = [exchanged(blocks[half * groups:(half + 1) * groups]) for half in range(halves)]
    known = [0] + order[:KNOWN] if groups > KNOWN + 1 else list(range(groups - 1))
    all_warp = jnp.concatenate([arrived[0][k][some * rank:some * rank + 1, :total] for k in known], axis=0)
    tiles, last_tiles = pl.pallas_call(
        functools.partial(tiles_kernel, part, bits, known),
        out_shape=[
            jax.ShapeDtypeStruct((group_bits, len(known) * part, rank, 2 * rank), bf16),
            jax.ShapeDtypeStruct((len(known) * part, rank, 2 * rank), bf16),
        ],
        in_specs=[VMEM, VMEM, VMEM],
        out_specs=[VMEM, VMEM],
        scratch_shapes=both_tables + [pltpu.VMEM((part, len(known), LANES), f32)],
        compiler_params=params,
        cost_estimate=cost(total // 2 * (group_bits + 1)),
        name="remote_tiles",
    )(all_warp, interp, omega)
    late_rows = pltpu.VMEM((groups - len(known), part, WARP_ROWS, LANES), f32)
    late = [arrived[0][k] for k in range(groups) if k not in known]
    returned = []
    for half in range(halves):
        state = pl.pallas_call(
            functools.partial(remote_kernel, groups, half * some, part, bits, known),
            out_shape=jax.ShapeDtypeStruct((groups * some, rank, width), bf16),
            in_specs=[VMEM] * (3 + groups + len(late)),
            out_specs=VMEM,
            scratch_shapes=both_tables + [late_rows],
            compiler_params=params,
            cost_estimate=cost(total // 2 // halves * group_bits),
            name=f"remote_{half}",
        )(tiles, interp, omega, *[arrived[half][k] for k in range(groups)], *late)
        other = lax.ppermute(state, "tgt", [(i, i ^ 1) for i in range(lax.axis_size("tgt"))])
        blocks = pl.pallas_call(
            functools.partial(core_kernel, groups, half * some, part, bits + group_bits, known),
            out_shape=[block] * groups,
            in_specs=[VMEM] * (5 + len(late)),
            out_specs=[VMEM] * groups,
            scratch_shapes=both_tables + [late_rows],
            compiler_params=params,
            cost_estimate=cost(total // 2 // halves),
            name=f"core_{half}",
        )(last_tiles, interp, omega, state, other, *late)
        returned.append(exchanged(blocks))
    values = None
    items = [(k, half) for half in range(halves) for k in [0] + order]
    cuts = [0, len(items) // 2, len(items) - len(order) // 2, len(items)]
    for i, (start, stop) in enumerate(zip(cuts, cuts[1:])):
        chosen = items[start:stop]
        operands = [warp, eval_interp, eval_omega] + [returned[half][k] for k, half in chosen]
        specs = [VMEM] * len(operands)
        aliases = {}
        if values is not None:
            aliases = {len(operands): 0}
            operands.append(values)
            specs.append(ANY)
        values = pl.pallas_call(
            functools.partial(eval_kernel, part, [(k, half * some) for k, half in chosen]),
            out_shape=jax.ShapeDtypeStruct((groups, part, rank, width), f32),
            in_specs=specs,
            out_specs=ANY,
            scratch_shapes=[
                pltpu.VMEM((len(chosen), some, rank, width), f32),
                pltpu.VMEM((total, LANES), f32),
                pltpu.SemaphoreType.DMA((len(chosen),)),
            ],
            input_output_aliases=aliases,
            compiler_params=params,
            cost_estimate=cost(len(chosen)),
            name=f"eval_{i}",
        )(*operands)
    return values.reshape(total, rank, width)


def solution(mesh):
    in_specs = (P(("grp", "src", "tgt"), None, None), P(("grp", "src", "tgt")), P(), P(), P(), P())
    out_specs = P(("grp", "src", "tgt"), None, None)
    return jax.shard_map(
        on_device, mesh=mesh, in_specs=in_specs, out_specs=out_specs, check_vma=False
    )
```

```python
import functools
import math

import jax
import jax.numpy as jnp
from jax import lax
from jax.experimental import pallas as pl
from jax.experimental.pallas import tpu as pltpu
from jax.sharding import PartitionSpec as P

KNOWN = 4
BATCH = 16
GROUP_BITS = 3
HALVES = 2
VMEM_LIMIT = 20 * 1024 * 1024
LOCAL_VMEM_LIMIT = 60 * 1024 * 1024
WARP_ROWS = 16
VMEM = pl.BlockSpec(memory_space=pltpu.VMEM)
ANY = pl.BlockSpec(memory_space=pl.ANY)
HBM = pl.BlockSpec(memory_space=pltpu.HBM)
SINE = (6.28318516, -41.34165503, 81.60100405, -76.54978181, 39.53670223)
LANES = 128


def cosine(turns):
    u = turns - jnp.round(turns)
    z = 0.25 - jnp.abs(u)
    v = z * z
    poly = SINE[-1]
    for coefficient in SINE[-2::-1]:
        poly = poly * v + coefficient
    return z * poly


def tile(gains, turns, scale):
    return (gains * cosine(turns * scale)).astype(jnp.bfloat16)


def product(tiles, state):
    return jnp.dot(tiles, state, preferred_element_type=jnp.float32)


def split_pair(index, bit):
    low = index & ((1 << bit) - 1)
    return ((index >> bit) << (bit + 1)) | low


def pairs_of(count, bit):
    firsts = [split_pair(i, bit) for i in range(count // 2)]
    return [(i, first, first | (1 << bit)) for i, first in enumerate(firsts)]


def multiply(pairs, tiles, load, store):
    for start in range(0, len(pairs), BATCH):
        batch = pairs[start:start + BATCH]
        states = [jnp.concatenate([load(first), load(second)], axis=0) for _, first, second in batch]
        results = [product(tiles(i), x).astype(jnp.bfloat16) for (i, _, _), x in zip(batch, states)]
        for (_, first, second), y in zip(batch, results):
            rank = y.shape[0] // 2
            store(first, y[:rank])
            store(second, y[rank:])


def stack_tables(interp_ref, omega_ref, gains, turns, flips):
    rank = interp_ref.shape[-1]
    for table, out, scale in ((interp_ref, gains, 1.0), (omega_ref, turns, 0.5 / math.pi)):
        for flip in range(flips):
            for row in range(2):
                child = row ^ flip
                for column in range(2):
                    part = table[child, row ^ column].astype(jnp.float32) * scale
                    out[flip, row * rank:(row + 1) * rank, column * rank:(column + 1) * rank] = part


def scale_rows(warp_ref, rows):
    count = rows.shape[0]
    warp = jnp.broadcast_to(warp_ref[...].astype(jnp.float32), (count, count))
    diagonal = lax.broadcasted_iota(jnp.int32, (count, count), 0) == lax.broadcasted_iota(jnp.int32, (count, count), 1)
    column = jnp.sum(jnp.where(diagonal, warp, 0.0), axis=1, keepdims=True)
    rows[...] = jnp.broadcast_to(column, rows.shape)


def local_kernel(groups, halves, group_bits, *refs):
    given, outs, rest = refs[:4], refs[4:4 + halves * groups], refs[4 + halves * groups:]
    warp_ref, interp_ref, omega_ref, state, gains, turns, rows, tiles, sems = rest
    copies = [pltpu.make_async_copy(src, dst, sems.at[i]) for i, (src, dst) in enumerate(zip(given, rest))]
    for copy in copies:
        copy.start()
    for copy in copies[:3]:
        copy.wait()
    stack_tables(interp_ref, omega_ref, gains, turns, 1)
    scale_rows(warp_ref, rows)
    total, rank, width = state.shape
    bits = total.bit_length() - 1
    place = lax.axis_index("src")

    def make_tiles(box):
        for child in range(2):
            half = slice(child * rank, (child + 1) * rank)
            wanted = [level for level in range(bits) if box >> level & 1 == child]
            if wanted:
                before, now = None, cosine(turns[0, half] * (rows[box:box + 1] * 0.25))
                twice = now + now
                for level in range(max(wanted) + 1):
                    if level:
                        before, now = now, twice * now - (1.0 if level == 1 else before)
                    if level in wanted:
                        low = box & ((1 << level) - 1)
                        tiles[level, ((box >> (level + 1)) << level) | low, half] = (gains[0, half] * now).astype(jnp.bfloat16)

    def load(box):
        return state[box]

    def store(box, y):
        state[box] = y

    def level_products(level, pairs):
        multiply(pairs, lambda i: tiles[level, i], load, store)

    size = 1 << group_bits
    for start in range(0, total + size, size):
        for box in range(start, min(start + size, total)):
            make_tiles(box)
        if start == 0:
            copies[3].wait()
        else:
            for level in range(group_bits):
                level_products(level, [p for p in pairs_of(total, level) if start - size <= p[1] < start])
    for level in range(group_bits, bits):
        level_products(level, pairs_of(total, level))

    part = total // groups
    warps = jnp.broadcast_to(warp_ref[...].astype(jnp.float32), (WARP_ROWS, total))
    warps = jnp.concatenate([warps, jnp.zeros((WARP_ROWS, width - total), jnp.float32)], axis=1).astype(jnp.bfloat16)
    some = part // halves
    for k in range(groups):
        for half in range(halves):
            out = outs[half * groups + k]
            out[:some * rank] = state[pl.ds((place ^ k) * part + half * some, some)].reshape(some * rank, width)
            if half == 0:
                out[some * rank:] = warps


def warp_rows(warps, place, part, rows):
    lanes = lax.broadcasted_iota(jnp.int32, warps.shape, 1)
    for m in range(part):
        column = jnp.sum(jnp.where(lanes == place * part + m, warps, 0.0), axis=1, keepdims=True)
        rows[m] = jnp.broadcast_to(column, rows.shape[1:])


def tiles_kernel(part, first_level, ks, warp_ref, interp_ref, omega_ref, tiles, last_tiles, gains, turns, rows):
    stack_tables(interp_ref, omega_ref, gains, turns, 2)
    rank = interp_ref.shape[-1]
    place, core = lax.axis_index("src"), lax.axis_index("tgt")
    warp_rows(warp_ref[...].astype(jnp.float32), place, part, rows)
    for j, k in enumerate(ks):
        for m in range(part):
            for step in range(tiles.shape[0]):
                side, s = place >> step & 1, k >> step & 1
                half = slice(s * rank, (s + 1) * rank)
                scale = rows[m, j:j + 1] * ((first_level + step + 1) / 4.0)
                tiles[step, j * part + m] = tile(gains[side, half], turns[side, half], scale)
            scale = rows[m, j:j + 1] * ((first_level + tiles.shape[0] + 1) / 4.0)
            last_tiles[j * part + m] = tile(gains[core, :rank], turns[core, :rank], scale)


def remote_kernel(groups, first_m, part, first_level, known, tiles, interp_ref, omega_ref, *rest):
    unknown = [k for k in range(groups) if k not in known]
    blocks, late, (out, gains, turns, rows) = rest[:groups], rest[groups:groups + len(unknown)], rest[groups + len(unknown):]
    stack_tables(interp_ref, omega_ref, gains, turns, 2)
    count, rank, width = out.shape
    some = count // groups
    some_bits = some.bit_length() - 1
    place = lax.axis_index("src")
    for j, ref in enumerate(late):
        warp_rows(ref[ref.shape[0] - WARP_ROWS:, :LANES].astype(jnp.float32), place, part, rows.at[j])
    for step in range(groups.bit_length() - 1):
        side = place >> step & 1

        def half_tile(i, step=step, side=side):
            k, m = i // some, first_m + i % some
            if k in known:
                return tiles[step, known.index(k) * part + m]
            scale = rows[unknown.index(k), m, :1] * ((first_level + step + 1) / 4.0)
            half = slice((k >> step & 1) * rank, ((k >> step & 1) + 1) * rank)
            return tile(gains[side, half], turns[side, half], scale)

        def load(i, step=step):
            m = i % some
            return out[i] if step else blocks[i // some][m * rank:(m + 1) * rank]

        def store(i, y):
            out[i] = y

        def tile_of(i, step=step, half_tile=half_tile):
            first = split_pair(i, step + some_bits)
            return jnp.concatenate([half_tile(first), half_tile(first | (1 << (step + some_bits)))], axis=0)

        multiply(pairs_of(count, step + some_bits), tile_of, load, store)


def core_kernel(groups, first_m, part, level, known, tiles, interp_ref, omega_ref, own, other, *rest):
    unknown = [k for k in range(groups) if k not in known]
    late, rest = rest[:len(unknown)], rest[len(unknown):]
    outs, (gains, turns, rows) = rest[:groups], rest[groups:]
    stack_tables(interp_ref, omega_ref, gains, turns, 2)
    rank = interp_ref.shape[-1]
    some = own.shape[0] // groups
    place, core = lax.axis_index("src"), lax.axis_index("tgt")
    for j, ref in enumerate(late):
        warp_rows(ref[ref.shape[0] - WARP_ROWS:, :LANES].astype(jnp.float32), place, part, rows.at[j])
    for k in range(groups):
        for m in range(some):
            x = jnp.concatenate([own[k * some + m], other[k * some + m]], axis=0)
            if k in known:
                tiles_m = tiles[known.index(k) * part + first_m + m]
            else:
                scale = rows[unknown.index(k), first_m + m, :1] * ((level + 1) / 4.0)
                tiles_m = tile(gains[core, :rank], turns[core, :rank], scale)
            outs[k][m * rank:(m + 1) * rank] = product(tiles_m, x).astype(jnp.bfloat16)


def eval_kernel(part, items, warp_ref, interp_ref, omega_ref, *rest):
    blocks = rest[:len(items)]
    out_hbm, values, rows, sems = rest[-4:]
    rank = interp_ref.shape[-1]
    some = blocks[0].shape[0] // rank
    place = lax.axis_index("src")
    scale_rows(warp_ref, rows)
    gains = interp_ref[...].astype(jnp.float32)
    turns = omega_ref[...] * (0.5 / math.pi)
    gains, turns = jnp.concatenate([gains, gains], axis=1), jnp.concatenate([turns, turns], axis=1)
    left = lax.broadcasted_iota(jnp.int32, (1, 2 * rank), 1) < rank
    copies = []
    for n, (k, first) in enumerate(items):
        group = place ^ k

        def scale_of(m):
            return rows[pl.ds(group * part + first + m, 1), :]

        for m in range(0, some, 2):
            if m + 1 < some:
                both = tile(gains, turns, jnp.where(left, scale_of(m), scale_of(m + 1)))
                none = jnp.zeros_like(both)
                tiles = jnp.concatenate([jnp.where(left, both, none), jnp.where(left, none, both)], axis=0)
                result = product(tiles, blocks[n][m * rank:(m + 2) * rank])
                values[n, m], values[n, m + 1] = result[:rank], result[rank:]
            else:
                tiles = tile(gains[:, :rank], turns[:, :rank], scale_of(m)[:, :rank])
                values[n, m] = product(tiles, blocks[n][m * rank:(m + 1) * rank])
        copy = pltpu.make_async_copy(values.at[n], out_hbm.at[group, first:first + some], sems.at[n])
        copy.start()
        copies.append(copy)
    for copy in copies:
        copy.wait()


def on_device(sources, warp, interp, omega, eval_interp, eval_omega):
    total, rank, width = sources.shape
    bits = total.bit_length() - 1
    groups = lax.axis_size("src")
    group_bits = groups.bit_length() - 1
    part = total // groups
    halves = min(HALVES, part)
    some = part // halves
    bf16, f32 = jnp.bfloat16, jnp.float32
    params = pltpu.CompilerParams(vmem_limit_bytes=VMEM_LIMIT)
    warp = warp.reshape(1, total)
    block = jax.ShapeDtypeStruct((some * rank, width), bf16)
    long_block = jax.ShapeDtypeStruct((some * rank + WARP_ROWS, width), bf16)
    both_tables = [pltpu.VMEM((2, 2 * rank, 2 * rank), f32)] * 2
    far, near = list(range(groups // 2, groups)), list(range(1, groups // 2))
    far_order, near_order = sorted(far, key=lambda k: (k & 1, k if k & 1 else -k)), sorted(near, key=lambda k: (k & 1, k))
    order = [k for pair in zip(far_order, near_order) for k in pair] + far_order[len(near):]

    def cost(steps):
        return pl.CostEstimate(flops=steps, bytes_accessed=steps, transcendentals=0)

    def after(value, done):
        return lax.optimization_barrier((value, done))[0]

    def moved(value, k):
        return lax.ppermute(value, "src", [(i, i ^ k) for i in range(groups)])

    blocks = pl.pallas_call(
        functools.partial(local_kernel, groups, halves, min(GROUP_BITS, bits)),
        out_shape=[long_block] * groups + [block] * ((halves - 1) * groups),
        in_specs=[HBM] * 4,
        out_specs=[VMEM] * (halves * groups),
        scratch_shapes=[
            pltpu.VMEM(warp.shape, warp.dtype),
            pltpu.VMEM(interp.shape, interp.dtype),
            pltpu.VMEM(omega.shape, omega.dtype),
            pltpu.VMEM((total, rank, width), bf16),
            pltpu.VMEM((1, 2 * rank, 2 * rank), f32),
            pltpu.VMEM((1, 2 * rank, 2 * rank), f32),
            pltpu.VMEM((total, LANES), f32),
            pltpu.VMEM((bits, total // 2, 2 * rank, 2 * rank), bf16),
            pltpu.SemaphoreType.DMA((4,)),
        ],
        compiler_params=pltpu.CompilerParams(vmem_limit_bytes=LOCAL_VMEM_LIMIT),
        cost_estimate=cost(total // 2 * bits),
        name="local",
    )(warp, interp, omega, sources)
    def exchanged(blocks):
        arrived = {0: blocks[0]}
        for k in order:
            arrived[k] = moved(blocks[k], k)
        return arrived

    arrived = [exchanged(blocks[half * groups:(half + 1) * groups]) for half in range(halves)]
    known = [0] + order[:KNOWN] if groups > KNOWN + 1 else list(range(groups - 1))
    all_warp = jnp.concatenate([arrived[0][k][some * rank:some * rank + 1, :total] for k in known], axis=0)
    tiles, last_tiles = pl.pallas_call(
        functools.partial(tiles_kernel, part, bits, known),
        out_shape=[
            jax.ShapeDtypeStruct((group_bits, len(known) * part, rank, 2 * rank), bf16),
            jax.ShapeDtypeStruct((len(known) * part, rank, 2 * rank), bf16),
        ],
        in_specs=[VMEM, VMEM, VMEM],
        out_specs=[VMEM, VMEM],
        scratch_shapes=both_tables + [pltpu.VMEM((part, len(known), LANES), f32)],
        compiler_params=params,
        cost_estimate=cost(total // 2 * (group_bits + 1)),
        name="remote_tiles",
    )(all_warp, interp, omega)
    late_rows = pltpu.VMEM((groups - len(known), part, WARP_ROWS, LANES), f32)
    late = [arrived[0][k] for k in range(groups) if k not in known]
    returned = []
    for half in range(halves):
        state = pl.pallas_call(
            functools.partial(remote_kernel, groups, half * some, part, bits, known),
            out_shape=jax.ShapeDtypeStruct((groups * some, rank, width), bf16),
            in_specs=[VMEM] * (3 + groups + len(late)),
            out_specs=VMEM,
            scratch_shapes=both_tables + [late_rows],
            compiler_params=params,
            cost_estimate=cost(total // 2 // halves * group_bits),
            name=f"remote_{half}",
        )(tiles, interp, omega, *[arrived[half][k] for k in range(groups)], *late)
        other = lax.ppermute(state, "tgt", [(i, i ^ 1) for i in range(lax.axis_size("tgt"))])
        blocks = pl.pallas_call(
            functools.partial(core_kernel, groups, half * some, part, bits + group_bits, known),
            out_shape=[block] * groups,
            in_specs=[VMEM] * (5 + len(late)),
            out_specs=[VMEM] * groups,
            scratch_shapes=both_tables + [late_rows],
            compiler_params=params,
            cost_estimate=cost(total // 2 // halves),
            name=f"core_{half}",
        )(last_tiles, interp, omega, state, other, *late)
        returned.append(exchanged(blocks))
    values = None
    items = [(k, half) for half in range(halves) for k in [0] + order]
    cuts = [0, len(items) // 2, len(items) - len(order) // 2, len(items)]
    for i, (start, stop) in enumerate(zip(cuts, cuts[1:])):
        chosen = items[start:stop]
        operands = [warp, eval_interp, eval_omega] + [returned[half][k] for k, half in chosen]
        specs = [VMEM] * len(operands)
        aliases = {}
        if values is not None:
            aliases = {len(operands): 0}
            operands.append(values)
            specs.append(ANY)
        values = pl.pallas_call(
            functools.partial(eval_kernel, part, [(k, half * some) for k, half in chosen]),
            out_shape=jax.ShapeDtypeStruct((groups, part, rank, width), f32),
            in_specs=specs,
            out_specs=ANY,
            scratch_shapes=[
                pltpu.VMEM((len(chosen), some, rank, width), f32),
                pltpu.VMEM((total, LANES), f32),
                pltpu.SemaphoreType.DMA((len(chosen),)),
            ],
            input_output_aliases=aliases,
            compiler_params=params,
            cost_estimate=cost(len(chosen)),
            name=f"eval_{i}",
        )(*operands)
    return values.reshape(total, rank, width)


def solution(mesh):
    in_specs = (P(("grp", "src", "tgt"), None, None), P(("grp", "src", "tgt")), P(), P(), P(), P())
    out_specs = P(("grp", "src", "tgt"), None, None)
    return jax.shard_map(
        on_device, mesh=mesh, in_specs=in_specs, out_specs=out_specs, check_vma=False
    )
```
